32 devices in a mesh: walk: 8 (over z, x), pan: 4 (over y, core).
Axes of the slice: x: 2, y: 2, z: 4, core: 2. Of those that a mesh axis runs over, the one named last changes fastest.
Arguments:
- dlog: bfloat16 [16384, 4096], P('walk', 'pan'), may hold values from 0 to 2
- dener: bfloat16 [16384, 4096], P('walk', 'pan'), may hold values from -0.5 to 2.5
- energy: float32 [16384], P('walk'), may hold values from -3 to -1
- mask: int32 [16], replicated, may hold values 0 or 1
- owner: int32 [16], replicated, may hold values from 0 to 15, each once
Outputs:
- correlation: float32 [4096, 4096], P('walk', 'pan')
- hamilton: float32 [4096, 4096], P('walk', 'pan')
The draws below stay inside these ranges and needn't reach their ends.
Inputs may be any that keep to these rules, and one draw needn't show every extreme that they name: `owner`: each block number appears once.
All inputs are finite; a program needn't handle non-finite values.
Results may differ from the reference program's by a relative error of at most 0.005.
Values may be sent and summed in bfloat16 or wider, within the bound.
No kernel may reach another device: no remote copies, remote signals or barrier semaphores. Data moves between devices by JAX's collectives and lax.ppermute only.
A program may use at most 128 MiB of HBM per device.

```python
import jax
import jax.numpy as jnp
from jax import lax

P_SIZE = 4096
BLOCK = 256
W = 16384
NB = 16


def set_ends(drawn, rng, least, top_value):
    extent = drawn.shape
    spot = [jax.random.randint(jax.random.fold_in(rng, axis), (), 0, extent[axis]) for axis in range(len(extent))]
    drawn = drawn.at[tuple(spot)].set(least)
    longest = extent.index(max(extent))
    spot[longest] = (spot[longest] + 1) % extent[longest]
    return drawn.at[tuple(spot)].set(top_value)


def block_scale(rng, extent, cuts, smallest, largest):
    factor_of, own = 1.0, jax.random.fold_in(rng, 6)
    for position, blocks in cuts:
        heights = jnp.exp(jax.random.uniform(jax.random.fold_in(own, position), (blocks,), jnp.float32, smallest / len(cuts), largest / len(cuts)))
        factor_of = factor_of * jnp.repeat(heights, extent[position] // blocks).reshape([-1 if axis == position else 1 for axis in range(len(extent))])
    return factor_of


def setup_inputs(seed: int = 0) -> dict:
    splits = jax.random.split(jax.random.key(seed), 6)
    dlog = jnp.clip(2.0 * jax.random.uniform(splits[0], (W, P_SIZE), jnp.float32) ** block_scale(splits[0], (W, P_SIZE), ((0, 8), (1, 4)), -0.2, 0.2), 0.0, 2.0).astype(jnp.bfloat16)
    dener = jnp.clip(-0.5 + 3.0 * jax.random.uniform(splits[1], (W, P_SIZE), jnp.float32) ** block_scale(splits[1], (W, P_SIZE), ((0, 8), (1, 4)), -0.2, 0.2), -0.5, 2.5).astype(jnp.bfloat16)
    energy = jnp.clip(-3.0 + 2.0 * jax.random.uniform(splits[2], (W,), jnp.float32) ** block_scale(splits[2], (W,), ((0, 8),), -0.2, 0.2), -3.0, -1.0)
    mask = set_ends((jax.random.randint(splits[3], (NB,), 0, 4) < 3).astype(jnp.int32), jax.random.fold_in(splits[3], 1), 0, 1)
    owner = jax.random.permutation(splits[4], NB).astype(jnp.int32)
    return dict(dlog=dlog, dener=dener, energy=energy, mask=mask, owner=owner)


def reference(dlog, dener, energy, mask, owner):
    total = dlog.shape[0]
    colmask = jnp.repeat(mask, BLOCK).astype(jnp.float32)
    om = dlog.astype(jnp.float32) * colmask
    gm = dener.astype(jnp.float32) * colmask
    obar = jnp.sum(om, 0) / total
    gbar = jnp.sum(gm, 0) / total
    ebar = jnp.sum(energy) / total
    ocf = om - obar
    oc = ocf.astype(jnp.bfloat16)
    hc = ((energy - ebar)[:, None] * ocf + gm - gbar).astype(jnp.bfloat16)
    ocp = jnp.take(oc.reshape(total, NB, BLOCK), owner, axis=1).reshape(total, P_SIZE)
    dims = (((0,), (0,)), ((), ()))
    correlation = lax.dot_general(ocp, oc, dims, preferred_element_type=jnp.float32) / total
    hamilton = lax.dot_general(ocp, hc, dims, preferred_element_type=jnp.float32) / total
    return correlation, hamilton
```

```python
import functools

import jax
import jax.numpy as jnp
from jax import lax
from jax.experimental import pallas as pl
from jax.experimental.pallas import tpu as pltpu
from jax.sharding import PartitionSpec as P

BLOCK = 256
SHIFT = -2.0
VMEM_LIMIT = 48 * 1024 * 1024
F32 = jnp.float32
BF16 = jnp.bfloat16
HIGHEST = lax.Precision.HIGHEST


def prepare_kernel(mask_ref, energy_ref, dlog_ref, dener_ref, oc_ref, hc_ref, stat_ref):
    on = mask_ref[pl.program_id(0)].astype(F32)
    rows = dlog_ref.shape[0]
    om = dlog_ref[...].astype(F32) * on
    gm = dener_ref[...].astype(F32) * on
    mu = jnp.sum(om, 0, keepdims=True) / rows
    gamma = jnp.sum(gm, 0, keepdims=True) / rows
    oc = om - mu
    turned = (energy_ref[...] - SHIFT) * oc
    oc_ref[...] = oc.astype(BF16)
    hc_ref[...] = (turned + gm - gamma).astype(BF16)
    stat_ref[0:1] = mu
    stat_ref[1:2] = gamma
    stat_ref[2:3] = jnp.sum(turned, 0, keepdims=True)
    stat_ref[3:8] = jnp.zeros((5, stat_ref.shape[1]), F32)


def prepare(local_mask, energy, dlog, dener):
    rows, width = dlog.shape
    block = pl.BlockSpec((rows, BLOCK), lambda t, m: (0, t))
    return pl.pallas_call(
        prepare_kernel,
        grid_spec=pltpu.PrefetchScalarGridSpec(
            num_scalar_prefetch=1,
            grid=(width // BLOCK,),
            in_specs=[pl.BlockSpec((rows, 1), lambda t, m: (0, 0)), block, block],
            out_specs=[block, block, pl.BlockSpec((8, BLOCK), lambda t, m: (0, t))],
        ),
        out_shape=[
            jax.ShapeDtypeStruct((rows, width), BF16),
            jax.ShapeDtypeStruct((rows, width), BF16),
            jax.ShapeDtypeStruct((8, width), F32),
        ],
        compiler_params=pltpu.CompilerParams(vmem_limit_bytes=VMEM_LIMIT),
        cost_estimate=pl.CostEstimate(flops=10 * rows * width, bytes_accessed=8 * rows * width, transcendentals=0),
        name="prepare",
    )(local_mask, energy[:, None], dlog, dener)


def product_kernel(plan, n_src, kind, where_ref, *refs):
    srcs, refs = refs[:n_src], refs[n_src:]
    oc_ref, hc_ref, refs = refs[0], refs[1], refs[2:]
    n_in = {"first": 0, "own": 0}.get(kind, 1)
    arrived, refs = refs[:n_in], refs[n_in:]
    n_out = 2 if kind == "first" else 1
    outs, (raw, turned, sem) = refs[:n_out], refs[n_out:]

    @pl.when(pl.program_id(0) == 0)
    def _():
        plan(where_ref, srcs, raw, sem)
        x = raw[...].astype(F32) * where_ref[3].astype(F32)
        x = x - jnp.sum(x, 0, keepdims=True) / x.shape[0]
        turned[...] = x.astype(BF16).T

    lhs = turned[...]
    c = jnp.dot(lhs, oc_ref[...], preferred_element_type=F32)
    h = jnp.dot(lhs, hc_ref[...], preferred_element_type=F32)
    if kind == "first":
        outs[0][...] = c.astype(outs[0].dtype)
        outs[1][...] = h.astype(outs[1].dtype)
        return
    out = outs[0]
    if kind == "add_c":
        c = c + arrived[0][...].astype(F32)
    elif kind == "add_h":
        h = h + arrived[0][...].astype(F32)
    elif kind == "add":
        c = c + arrived[0][0].astype(F32)
        h = h + arrived[0][1].astype(F32)
    out[0] = c.astype(out.dtype)
    out[1] = h.astype(out.dtype)


def product(plan, where, srcs, oc, hc, kind, arrived=()):
    rows, width = oc.shape
    tile = min(512, width)
    cols = pl.BlockSpec((rows, tile), lambda t, s: (0, t))
    one = pl.BlockSpec((BLOCK, tile), lambda t, s: (0, t))
    two = pl.BlockSpec((2, BLOCK, tile), lambda t, s: (0, 0, t))
    in_specs = [pl.BlockSpec(memory_space=pl.ANY)] * len(srcs) + [cols, cols]
    in_specs += [two if a.ndim == 3 else one for a in arrived]
    if kind == "first":
        out_specs = [one, one]
        out_shape = [jax.ShapeDtypeStruct((BLOCK, width), BF16)] * 2
    else:
        out_specs = two
        out_shape = jax.ShapeDtypeStruct((2, BLOCK, width), F32 if kind == "own" else BF16)
    return pl.pallas_call(
        functools.partial(product_kernel, plan, len(srcs), kind),
        grid_spec=pltpu.PrefetchScalarGridSpec(
            num_scalar_prefetch=1,
            grid=(width // tile,),
            in_specs=in_specs,
            out_specs=out_specs,
            scratch_shapes=[
                pltpu.VMEM((rows, BLOCK), BF16),
                pltpu.VMEM((BLOCK, rows), BF16),
                pltpu.SemaphoreType.DMA((2,)),
            ],
        ),
        out_shape=out_shape,
        compiler_params=pltpu.CompilerParams(vmem_limit_bytes=VMEM_LIMIT),
        cost_estimate=pl.CostEstimate(
            flops=4 * BLOCK * rows * width, bytes_accessed=4 * rows * width + 4 * BLOCK * width, transcendentals=0
        ),
        name="product_" + kind,
    )(where, *srcs, oc, hc, *arrived)


def fetch_whole(where_ref, srcs, raw, sem):
    start = pl.multiple_of(where_ref[1] * BLOCK, BLOCK)
    copy = pltpu.make_async_copy(srcs[0].at[:, pl.ds(start, BLOCK)], raw, sem.at[0])
    copy.start()
    copy.wait()


def fetch_parts(where_ref, srcs, raw, sem):
    half = raw.shape[0] // 2
    core = where_ref[2]
    near = pl.ds(pl.multiple_of(core * half, half), half)
    far = pl.ds(pl.multiple_of((1 - core) * half, half), half)
    cols = pl.ds(pl.multiple_of(where_ref[1] * BLOCK, BLOCK), BLOCK)

    def bring(near_src, far_src):
        one = pltpu.make_async_copy(near_src, raw.at[near], sem.at[0])
        two = pltpu.make_async_copy(far_src, raw.at[far], sem.at[1])
        one.start()
        two.start()
        one.wait()
        two.wait()

    @pl.when(where_ref[0] == 0)
    def _():
        bring(srcs[0].at[near, cols], srcs[0].at[far, cols])

    @pl.when(where_ref[0] == 1)
    def _():
        bring(srcs[1].at[:, cols], srcs[2].at[:, cols])

    for t in range((len(srcs) - 3) // 2):

        @pl.when(where_ref[0] == 2 + t)
        def _(t=t):
            bring(srcs[3 + 2 * t], srcs[4 + 2 * t])


def after(value, *others):
    return lax.optimization_barrier((value, *others))[0]


def per_device(dlog, dener, energy, mask, owner):
    wdev, width = dlog.shape
    nwalk, npan = lax.axis_size("walk"), lax.axis_size("pan")
    total = wdev * nwalk
    full = width * npan
    nblocks = full // BLOCK
    mine = width // BLOCK
    per_dest = nblocks // nwalk
    half = nwalk // 2
    pan, walk = lax.axis_index("pan"), lax.axis_index("walk")

    ring = [2 * k for k in range(half)] + [2 * k + 1 for k in reversed(range(half))]
    right = [(ring[k], ring[(k + 1) % nwalk]) for k in range(nwalk)]
    left = [(b, a) for a, b in right]
    spot = jnp.where(walk % 2 == 0, walk // 2, nwalk - 1 - walk // 2)

    offsets = [(half, k) for k in range(per_dest)]
    for j in range(half - 1, 0, -1):
        for k in range(per_dest):
            offsets += [(j, k), (-j, k)]
    offsets += [(0, k) for k in range(per_dest)]
    goal = (spot + jnp.array([o for o, _ in offsets], jnp.int32)) % nwalk
    goal = jnp.where(goal < half, 2 * goal, 2 * (nwalk - 1 - goal) + 1)
    position = goal * per_dest + jnp.array([k for _, k in offsets], jnp.int32)
    wanted = owner[position]
    shown = mask[wanted]

    local_mask = lax.dynamic_slice_in_dim(mask, pan * mine, mine)

    if npan == 4:
        chip, core = pan // 2, pan % 2
        swap = [(j, j ^ 1) for j in range(npan)]
        cross = [(j, j ^ 2) for j in range(npan)]
        hrows = wdev // 2
        rounds = 2 * mine
        own_near = lax.dynamic_slice_in_dim(dlog, core * hrows, hrows)
        own_far = lax.dynamic_slice_in_dim(dlog, (1 - core) * hrows, hrows)
        sib_near = lax.ppermute(own_far, "pan", swap)
        sib_far = lax.ppermute(after(own_near, sib_near), "pan", swap)
        here = wanted // (2 * mine) == chip
        rank_here = jnp.cumsum(here) - 1
        rank_there = jnp.cumsum(~here) - 1
        ids = jnp.arange(nblocks)
        parts, got = [], []
        for t in range(rounds):
            block = jnp.sum(jnp.where(here & (rank_here == t), wanted, 0))
            ours = block // mine == pan
            at = (block % mine) * BLOCK
            a = lax.dynamic_slice_in_dim(own_near, at, BLOCK, 1)
            b = lax.dynamic_slice_in_dim(sib_near, at, BLOCK, 1)
            send = jnp.where(ours, a, b)
            if t >= 2:
                send = after(send, got[t - 2])
            got.append(lax.ppermute(send, "pan", cross))
            parts += [got[t], lax.ppermute(got[t], "pan", swap)]
        kind = jnp.where(here, jnp.where(wanted // mine == pan, 0, 1), 2 + rank_there)
        where = jnp.stack([kind, wanted % mine, jnp.full_like(wanted, core), shown], 1).astype(jnp.int32)
        plan = fetch_parts

        def sources(m):
            return [dlog, sib_near, sib_far] + parts[: 2 * min(m + 1, rounds)]
    else:
        gathered = lax.all_gather(dlog, "pan", axis=1, tiled=True)
        where = jnp.stack([wanted, wanted, wanted, shown], 1).astype(jnp.int32)
        plan = fetch_whole

        def sources(m):
            return [gathered]

    oc, hc, stats = prepare(local_mask, energy, dlog, dener)
    esum = jnp.sum(energy)
    stats = lax.dynamic_update_slice(stats, jnp.full((1, width), esum, F32), (3, 0))
    stats = stats[:4]
    table = lax.all_gather(lax.all_gather(stats, "pan", axis=1, tiled=True), "walk", axis=0)

    index = {key: m for m, key in enumerate(offsets)}

    def run(key, kind, *arrived):
        m = index[key]
        return product(plan, where[m], sources(m), oc, hc, kind, arrived)

    moving_right, moving_left = {}, {}
    for k in range(per_dest):
        c, h = run((half, k), "first")
        moving_right[k] = lax.ppermute(c, "walk", right)
        moving_left[k] = lax.ppermute(h, "walk", left)
    for j in range(half - 1, 0, -1):
        first = j == half - 1
        for k in range(per_dest):
            s = run((j, k), "add_c" if first else "add", moving_right[k])
            moving_right[k] = lax.ppermute(s, "walk", right)
            s = run((-j, k), "add_h" if first else "add", moving_left[k])
            moving_left[k] = lax.ppermute(s, "walk", left)
    own = [run((0, k), "own") for k in range(per_dest)]

    mu, gamma, q, esums = table[:, 0], table[:, 1], table[:, 2], table[:, 3, :1]
    ebar = jnp.sum(esums) / total
    delta = mu - jnp.mean(mu, 0)
    gdelta = gamma - jnp.mean(gamma, 0)
    mixed = q + (esums - SHIFT * wdev) * delta + wdev * gdelta

    def local_cols(x):
        return lax.dynamic_slice_in_dim(x, pan * width, width, 1)

    c_out, h_out = [], []
    for k in range(per_dest):
        block = owner[walk * per_dest + k]
        dl = lax.dynamic_slice_in_dim(delta, block * BLOCK, BLOCK, 1)
        ql = lax.dynamic_slice_in_dim(q, block * BLOCK, BLOCK, 1)
        dims = (((0,), (0,)), ((), ()))
        c_fix = lax.dot_general(dl * wdev, local_cols(delta), dims, precision=HIGHEST)
        h_fix = lax.dot_general(
            jnp.concatenate([ql, dl]), jnp.concatenate([local_cols(delta), local_cols(mixed)]), dims, precision=HIGHEST
        )
        c_out.append(own[k][0] + c_fix + (moving_right[k][0].astype(F32) + moving_left[k][0].astype(F32)))
        h_out.append(own[k][1] + h_fix + (moving_right[k][1].astype(F32) + moving_left[k][1].astype(F32)))
    c_all = jnp.concatenate(c_out) / total
    h_all = jnp.concatenate(h_out) / total + (SHIFT - ebar) * c_all
    return c_all, h_all


def solution(mesh):
    return jax.shard_map(
        per_device,
        mesh=mesh,
        in_specs=(P("walk", "pan"), P("walk", "pan"), P("walk"), P(), P()),
        out_specs=(P("walk", "pan"), P("walk", "pan")),
        check_vma=False,
    )
```

```python
import functools

import jax
import jax.numpy as jnp
from jax import lax
from jax.experimental import pallas as pl
from jax.experimental.pallas import tpu as pltpu
from jax.sharding import PartitionSpec as P

BLOCK = 256
VMEM_LIMIT = 56 * 1024 * 1024
F32 = jnp.float32
BF16 = jnp.bfloat16
PARAMS = pltpu.CompilerParams(vmem_limit_bytes=VMEM_LIMIT)
SMALL = pltpu.CompilerParams(vmem_limit_bytes=32 * 1024 * 1024)
HBM = pl.BlockSpec(memory_space=pltpu.HBM)
VMEM = pl.BlockSpec(memory_space=pltpu.VMEM)


def cost(flops, moved):
    return pl.CostEstimate(flops=flops // 100, bytes_accessed=moved // 100, transcendentals=0)


def sums_kernel(mask_ref, place_ref, energy_ref, dlog_ref, dener_ref, out_ref):
    on = mask_ref[place_ref[0] + pl.program_id(0)].astype(F32)
    out_ref[0:1] = jnp.sum(dlog_ref[...].astype(F32) * on, 0, keepdims=True)
    out_ref[1:2] = jnp.sum(dener_ref[...].astype(F32) * on, 0, keepdims=True)
    out_ref[2:8] = jnp.full((6, out_ref.shape[1]), jnp.sum(energy_ref[...]), F32)


def column_sums(mask, place, energy, dlog, dener):
    rows, width = dlog.shape
    block = pl.BlockSpec((rows, BLOCK), lambda t, *_: (0, t))
    energy = energy.reshape(rows // 128, 128)
    return pl.pallas_call(
        sums_kernel,
        grid_spec=pltpu.PrefetchScalarGridSpec(
            num_scalar_prefetch=2,
            grid=(width // BLOCK,),
            in_specs=[pl.BlockSpec(energy.shape, lambda t, *_: (0, 0)), block, block],
            out_specs=pl.BlockSpec((8, BLOCK), lambda t, *_: (0, t)),
        ),
        out_shape=jax.ShapeDtypeStruct((8, width), F32),
        compiler_params=PARAMS,
        cost_estimate=cost(4 * rows * width, 4 * rows * width),
        name="column_sums",
    )(mask, place, energy, dlog, dener)


def pack_kernel(turns, pick_ref, dlog_ref, sib_ref, *refs):
    n = len(turns)
    outs, (held, sem_in, sem_out) = refs[:n], refs[n:]
    half = held.shape[1]
    near = pl.ds(pl.multiple_of(pick_ref[0] * half, half), half)
    for i, t in enumerate(turns):
        cols = pl.ds(pl.multiple_of(pick_ref[2 * t + 2] * BLOCK, BLOCK), BLOCK)

        @pl.when(pick_ref[2 * t + 1] == 0)
        def _(i=i, cols=cols):
            pltpu.make_async_copy(dlog_ref.at[near, cols], held.at[i], sem_in.at[i]).start()

        @pl.when(pick_ref[2 * t + 1] != 0)
        def _(i=i, cols=cols):
            pltpu.make_async_copy(sib_ref.at[near, cols], held.at[i], sem_in.at[i]).start()

    for i in range(n):
        pltpu.make_async_copy(sib_ref.at[near, pl.ds(0, BLOCK)], held.at[i], sem_in.at[i]).wait()
        pltpu.make_async_copy(held.at[i], outs[i], sem_out.at[i]).start()
    for i in range(n):
        pltpu.make_async_copy(held.at[i], outs[i], sem_out.at[i]).wait()


def pack(pick, dlog, sib, turns):
    half = dlog.shape[0] // 2
    n = len(turns)
    return pl.pallas_call(
        functools.partial(pack_kernel, turns),
        in_specs=[pl.BlockSpec(memory_space=pltpu.SMEM), HBM, HBM],
        out_specs=[HBM] * n,
        out_shape=[jax.ShapeDtypeStruct((half, BLOCK), BF16)] * n,
        scratch_shapes=[
            pltpu.VMEM((n, half, BLOCK), BF16),
            pltpu.SemaphoreType.DMA((n,)),
            pltpu.SemaphoreType.DMA((n,)),
        ],
        compiler_params=PARAMS,
        cost_estimate=cost(0, 4 * n * half * BLOCK),
        name="pack",
    )(pick, dlog, sib)


WORDS = 5


def fetch_whole(row, srcs, raw, sem, n):
    cols = pl.ds(pl.multiple_of(row(1) * BLOCK, BLOCK), BLOCK)
    copy = pltpu.make_async_copy(srcs[0].at[:, cols], raw.at[n], sem.at[2 * n])
    copy.start()
    return [copy]


def fetch_parts(row, srcs, raw, sem, n):
    half = raw.shape[1] // 2
    core = row(2)
    near = pl.ds(pl.multiple_of(core * half, half), half)
    far = pl.ds(pl.multiple_of((1 - core) * half, half), half)
    cols = pl.ds(pl.multiple_of(row(1) * BLOCK, BLOCK), BLOCK)

    def bring(near_src, far_src):
        pltpu.make_async_copy(near_src, raw.at[n, near], sem.at[2 * n]).start()
        pltpu.make_async_copy(far_src, raw.at[n, far], sem.at[2 * n + 1]).start()

    @pl.when(row(0) == 0)
    def _():
        bring(srcs[0].at[near, cols], srcs[0].at[far, cols])

    @pl.when(row(0) == 1)
    def _():
        bring(srcs[1].at[near, cols], srcs[1].at[far, cols])

    for t in range((len(srcs) - 2) // 2):

        @pl.when(row(0) == 2 + t)
        def _(t=t):
            bring(srcs[2 + 2 * t], srcs[3 + 2 * t])

    some = srcs[1].at[pl.ds(0, half), pl.ds(0, BLOCK)]
    return [
        pltpu.make_async_copy(some, raw.at[n, pl.ds(0, half)], sem.at[2 * n]),
        pltpu.make_async_copy(some, raw.at[n, pl.ds(half, half)], sem.at[2 * n + 1]),
    ]


def turn(plan, total, where_ref, at, srcs, sums, raw, turned, sem):
    waits = [plan(lambda w, m=m: where_ref[m * WORDS + w], srcs, raw, sem, n) for n, m in enumerate(at)]
    for n, m in enumerate(at):
        for wait in waits[n]:
            wait.wait()
        x = raw[n].astype(F32) * where_ref[m * WORDS + 3].astype(F32) - sums[n][0] / total
        turned[n * BLOCK : (n + 1) * BLOCK] = x.astype(BF16).T


def prepare_kernel(plan, total, n_src, at, where_ref, mask_ref, place_ref, own_ref, *refs):
    srcs, refs = refs[:n_src], refs[n_src:]
    energy_ref, sums_ref, dlog_ref, dener_ref, oc_ref, hc_ref, c_ref, h_ref, raw, turned, sem = refs
    t = pl.program_id(0)

    @pl.when(t == 0)
    def _():
        turn(plan, total, where_ref, [at], srcs, [own_ref], raw, turned, sem)

    on = mask_ref[place_ref[0] + t].astype(F32)
    cols = pl.ds(pl.multiple_of(t * BLOCK, BLOCK), BLOCK)
    ocf = dlog_ref[...].astype(F32) * on - sums_ref[0:1] / total
    oc = ocf.astype(BF16)
    shift = energy_ref[...] - sums_ref[2:3, 0:1] / total
    hc = (shift * ocf + dener_ref[...].astype(F32) * on - sums_ref[1:2] / total).astype(BF16)
    oc_ref[:, cols] = oc
    hc_ref[:, cols] = hc
    c_ref[...] = jnp.dot(turned[...], oc, preferred_element_type=F32).astype(BF16)
    h_ref[...] = jnp.dot(turned[...], hc, preferred_element_type=F32).astype(BF16)


def scratch(n_pos, rows):
    return [
        pltpu.VMEM((n_pos, rows, BLOCK), BF16),
        pltpu.VMEM((n_pos * BLOCK, rows), BF16),
        pltpu.SemaphoreType.DMA((2 * n_pos,)),
    ]


def prepare(plan, total, where, at, table, srcs, mask, place, energy, sums, dlog, dener):
    rows, width = dlog.shape
    block = pl.BlockSpec((rows, BLOCK), lambda t, *_: (0, t))
    one = pl.BlockSpec((BLOCK, BLOCK), lambda t, *_: (0, t))
    in_specs = [pl.BlockSpec((1, 1, BLOCK), lambda t, s, *_: (s[at * WORDS + 4], 0, 0))] + [HBM] * len(srcs)
    in_specs += [pl.BlockSpec((rows, 1), lambda t, *_: (0, 0))]
    in_specs += [pl.BlockSpec((sums.shape[0], BLOCK), lambda t, *_: (0, t))]
    return pl.pallas_call(
        functools.partial(prepare_kernel, plan, total, len(srcs), at),
        grid_spec=pltpu.PrefetchScalarGridSpec(
            num_scalar_prefetch=3,
            grid=(width // BLOCK,),
            in_specs=in_specs + [block, block],
            out_specs=[VMEM, VMEM, one, one],
            scratch_shapes=scratch(1, rows),
        ),
        out_shape=[jax.ShapeDtypeStruct((rows, width), BF16)] * 2 + [jax.ShapeDtypeStruct((BLOCK, width), BF16)] * 2,
        compiler_params=SMALL,
        cost_estimate=cost(4 * BLOCK * rows * width, 8 * rows * width),
        name="prepare",
    )(where, mask, place, table, *srcs, energy, sums, dlog, dener)


def product_kernel(plan, total, n_src, at, kind, where_ref, *refs):
    n_pos = len(at)
    sums, srcs, refs = refs[:n_pos], refs[n_pos : n_pos + n_src], refs[n_pos + n_src :]
    oc_ref, hc_ref, refs = refs[0], refs[1], refs[2:]
    n_in = 0 if kind in ("first", "own") else n_pos
    arrived, refs = refs[:n_in], refs[n_in:]
    outs, (raw, turned, sem) = refs[:-3], refs[-3:]

    turn(plan, total, where_ref, at, srcs, sums, raw, turned, sem)
    lhs = turned[...]
    width = oc_ref.shape[1]
    tile = min(512, width)
    for start in range(0, width, tile):
        cols = slice(start, start + tile)
        c = jnp.dot(lhs, oc_ref[:, cols], preferred_element_type=F32)
        h = jnp.dot(lhs, hc_ref[:, cols], preferred_element_type=F32)
        if kind == "first":
            outs[0][:, cols] = c.astype(BF16)
            outs[1][:, cols] = h.astype(BF16)
            continue
        for n in range(n_pos):
            cn, hn = c[n * BLOCK : (n + 1) * BLOCK], h[n * BLOCK : (n + 1) * BLOCK]
            if kind == "add_c" or (kind == "second" and n == 0):
                cn = cn + arrived[n][:, cols].astype(F32)
            elif kind in ("add_h", "second"):
                hn = hn + arrived[n][:, cols].astype(F32)
            elif kind == "add":
                cn = cn + arrived[n][0, :, cols].astype(F32)
                hn = hn + arrived[n][1, :, cols].astype(F32)
            outs[n][0, :, cols] = cn.astype(outs[n].dtype)
            outs[n][1, :, cols] = hn.astype(outs[n].dtype)


def product(plan, total, where, at, table, srcs, oc, hc, kind, arrived=()):
    rows, width = oc.shape
    n_pos = len(at)
    in_specs = [pl.BlockSpec((1, 1, BLOCK), lambda t, s, m=m: (s[m * WORDS + 4], 0, 0)) for m in at]
    in_specs += [HBM] * len(srcs) + [VMEM] * (2 + len(arrived))
    if kind == "first":
        out_shape = [jax.ShapeDtypeStruct((BLOCK, width), BF16)] * 2
    else:
        out_shape = [jax.ShapeDtypeStruct((2, BLOCK, width), F32 if kind == "own" else BF16)] * n_pos
    return pl.pallas_call(
        functools.partial(product_kernel, plan, total, len(srcs), at, kind),
        grid_spec=pltpu.PrefetchScalarGridSpec(
            num_scalar_prefetch=1,
            grid=(1,),
            in_specs=in_specs,
            out_specs=[VMEM] * len(out_shape),
            scratch_shapes=scratch(n_pos, rows),
        ),
        out_shape=out_shape,
        compiler_params=SMALL,
        cost_estimate=cost(4 * n_pos * BLOCK * rows * width, 4 * rows * width + 8 * n_pos * BLOCK * width),
        name="product_" + kind,
    )(where, *[table] * n_pos, *srcs, oc, hc, *arrived)


def finish_kernel(total, own_ref, right_ref, left_ref, *refs):
    c_ref, h_ref = refs[-2:]
    c_ref[...] = (own_ref[0] + right_ref[0].astype(F32) + left_ref[0].astype(F32)) * (1.0 / total)
    h_ref[...] = (own_ref[1] + right_ref[1].astype(F32) + left_ref[1].astype(F32)) * (1.0 / total)


def finish(total, k, per_dest, own, right, left, so_far):
    _, rows, width = own.shape
    part = min(128, rows)
    two = pl.BlockSpec((2, part, width), lambda t: (0, t, 0))
    out = pl.BlockSpec((part, width), lambda t: (k * (rows // part) + t, 0))
    return pl.pallas_call(
        functools.partial(finish_kernel, total),
        grid=(rows // part,),
        in_specs=[two] * 3 + [HBM] * len(so_far),
        out_specs=[out, out],
        out_shape=[jax.ShapeDtypeStruct((per_dest * rows, width), F32)] * 2,
        input_output_aliases={3 + n: n for n in range(len(so_far))},
        compiler_params=PARAMS,
        cost_estimate=cost(6 * rows * width, 24 * rows * width),
        name="finish",
    )(own, right, left, *so_far)


def after(value, *others):
    return lax.optimization_barrier((value, *others))[0]


def sum_over_walk(x, nwalk, ties=()):
    if nwalk & (nwalk - 1):
        return lax.psum(x, "walk")
    step = 1
    while step < nwalk:
        if ties:
            x, ties = after(x, *ties[0]), ties[1:]
        x = x + lax.ppermute(x, "walk", [(w, w ^ step) for w in range(nwalk)])
        step *= 2
    return x


def per_device(dlog, dener, energy, mask, owner):
    wdev, width = dlog.shape
    nwalk, npan = lax.axis_size("walk"), lax.axis_size("pan")
    total = wdev * nwalk
    full = width * npan
    nblocks = full // BLOCK
    mine = width // BLOCK
    per_dest = nblocks // nwalk
    half = nwalk // 2
    pan, walk = lax.axis_index("pan"), lax.axis_index("walk")

    ring = [2 * k for k in range(half)] + [2 * k + 1 for k in reversed(range(half))]
    right = [(ring[k], ring[(k + 1) % nwalk]) for k in range(nwalk)]
    left = [(b, a) for a, b in right]
    spot = jnp.where(walk % 2 == 0, walk // 2, nwalk - 1 - walk // 2)

    offsets = [(half, k) for k in range(per_dest)]
    for j in range(half - 1, 0, -1):
        for k in range(per_dest):
            offsets += [(j, k), (-j, k)]
    offsets += [(0, k) for k in range(per_dest)]
    goal = (spot + jnp.array([o for o, _ in offsets], jnp.int32)) % nwalk
    goal = jnp.where(goal < half, 2 * goal, 2 * (nwalk - 1 - goal) + 1)
    position = goal * per_dest + jnp.array([k for _, k in offsets], jnp.int32)
    wanted = owner[position]
    shown = mask[wanted]
    place = (pan * mine)[None].astype(jnp.int32)
    column = energy[:, None]
    made = []

    if npan == 4:
        chip, core = pan // 2, pan % 2
        swap = [(j, j ^ 1) for j in range(npan)]
        cross = [(j, j ^ 2) for j in range(npan)]
        rounds = 2 * mine
        sib = lax.ppermute(dlog, "pan", swap)
        here = wanted // rounds == chip
        rank_here = jnp.cumsum(here) - 1
        rank_there = jnp.cumsum(~here) - 1
        turns = jnp.arange(rounds)[:, None]
        picked = jnp.sum(jnp.where(here & (rank_here == turns), wanted, 0), 1)
        pick = jnp.stack([jnp.where(picked // mine == pan, 0, 1), picked % mine], 1).reshape(-1)
        pick = jnp.concatenate([core[None], pick]).astype(jnp.int32)
        sums = column_sums(mask, after(place, pick), energy, dlog, dener)
        sums = jnp.concatenate([sums[:3], lax.ppermute(sums[:1], "pan", cross)])
        sends = pack(after(pick, sums), dlog, sib, tuple(range(rounds)))
        crossed = [lax.ppermute(send, "pan", cross) for send in sends]
        sums = sum_over_walk(sums, nwalk, [crossed[:1], (), crossed[1:2]])
        pair = jnp.stack([sums[0], sums[3]])
        table = jnp.concatenate([pair, lax.ppermute(pair, "pan", swap)])
        there = wanted // mine
        entry = ((there % 2 != core) * 2 + (there // 2 != chip)) * mine + wanted % mine
        kind = jnp.where(here, jnp.where(wanted // mine == pan, 0, 1), 2 + rank_there)
        where = jnp.stack([kind, wanted % mine, jnp.full_like(wanted, core), shown, entry], 1)
        plan = fetch_parts
        parts = []

        def sources(m):
            for t in range(len(parts) // 2, min(m + 1, rounds)):
                tie = {0: None, 1: table}.get(t, made[max(t - 2, 0)] if t >= 2 else None)
                got = crossed[t] if tie is None else after(crossed[t], tie)
                parts.extend([got, lax.ppermute(got, "pan", swap)])
            return [dlog, sib] + parts[: 2 * min(m + 1, rounds)]
    else:
        gathered = lax.all_gather(dlog, "pan", axis=1, tiled=True)
        sums = sum_over_walk(column_sums(mask, place, energy, dlog, dener), nwalk)
        table = lax.all_gather(sums[0], "pan")
        where = jnp.stack([wanted, wanted, wanted, shown, wanted], 1)
        plan = fetch_whole

        def sources(m):
            return [gathered]

    where = where.astype(jnp.int32).reshape(-1)
    table = table.reshape(nblocks, 1, BLOCK)
    oc, hc, first_c, first_h = prepare(
        plan, total, where, 0, table, sources(0), mask, place, column, sums, dlog, dener
    )
    made.append(first_c)
    index = {key: m for m, key in enumerate(offsets)}

    def run(keys, kind, *arrived):
        at = [index[key] for key in keys]
        outs = product(plan, total, where, at, table, sources(max(at)), oc, hc, kind, arrived)
        made.extend(outs[: len(at)])
        return outs

    moving_right, moving_left = {}, {}
    for k in range(per_dest):
        c, h = run([(half, k)], "first") if k else (first_c, first_h)
        moving_right[k] = lax.ppermute(c, "walk", right)
        moving_left[k] = lax.ppermute(h, "walk", left)
    for j in range(half - 1, 0, -1):
        for k in range(per_dest):
            one = j == half - 1
            if index[j, k] < 2 * mine:
                (r,) = run([(j, k)], "add_c" if one else "add", moving_right[k])
                moving_right[k] = lax.ppermute(r, "walk", right)
                (l,) = run([(-j, k)], "add_h" if one else "add", moving_left[k])
                moving_left[k] = lax.ppermute(l, "walk", left)
            else:
                r, l = run([(j, k), (-j, k)], "second" if one else "add", moving_right[k], moving_left[k])
                moving_right[k] = lax.ppermute(r, "walk", right)
                moving_left[k] = lax.ppermute(l, "walk", left)
    own = run([(0, k) for k in range(per_dest)], "own")
    outs = ()
    for k in range(per_dest):
        outs = finish(total, k, per_dest, own[k], moving_right[k], moving_left[k], outs)
    return tuple(outs)


def solution(mesh):
    return jax.shard_map(
        per_device,
        mesh=mesh,
        in_specs=(P("walk", "pan"), P("walk", "pan"), P("walk"), P(), P()),
        out_specs=(P("walk", "pan"), P("walk", "pan")),
        check_vma=False,
    )
```

```python
import functools

import jax
import jax.numpy as jnp
from jax import lax
from jax.experimental import pallas as pl
from jax.experimental.pallas import tpu as pltpu
from jax.sharding import PartitionSpec as P

BLOCK = 256
VMEM_LIMIT = 56 * 1024 * 1024
F32 = jnp.float32
BF16 = jnp.bfloat16
PARAMS = pltpu.CompilerParams(vmem_limit_bytes=VMEM_LIMIT)
SMALL = pltpu.CompilerParams(vmem_limit_bytes=32 * 1024 * 1024)
HBM = pl.BlockSpec(memory_space=pltpu.HBM)
VMEM = pl.BlockSpec(memory_space=pltpu.VMEM)


def cost(flops, moved):
    return pl.CostEstimate(flops=flops // 100, bytes_accessed=moved // 100, transcendentals=0)


def sums_kernel(mask_ref, place_ref, energy_ref, dlog_ref, dener_ref, out_ref):
    on = mask_ref[place_ref[0] + pl.program_id(0)].astype(F32)
    out_ref[0:1] = jnp.sum(dlog_ref[...].astype(F32) * on, 0, keepdims=True)
    out_ref[1:2] = jnp.sum(dener_ref[...].astype(F32) * on, 0, keepdims=True)
    out_ref[2:8] = jnp.full((6, out_ref.shape[1]), jnp.sum(energy_ref[...]), F32)


def column_sums(mask, place, energy, dlog, dener):
    rows, width = dlog.shape
    block = pl.BlockSpec((rows, BLOCK), lambda t, *_: (0, t))
    energy = energy.reshape(rows // 128, 128)
    return pl.pallas_call(
        sums_kernel,
        grid_spec=pltpu.PrefetchScalarGridSpec(
            num_scalar_prefetch=2,
            grid=(width // BLOCK,),
            in_specs=[pl.BlockSpec(energy.shape, lambda t, *_: (0, 0)), block, block],
            out_specs=pl.BlockSpec((8, BLOCK), lambda t, *_: (0, t)),
        ),
        out_shape=jax.ShapeDtypeStruct((8, width), F32),
        compiler_params=PARAMS,
        cost_estimate=cost(4 * rows * width, 4 * rows * width),
        name="column_sums",
    )(mask, place, energy, dlog, dener)


def pack_kernel(turns, pick_ref, dlog_ref, sib_ref, *refs):
    n = len(turns)
    outs, (held, sem_in, sem_out) = refs[:n], refs[n:]
    half = held.shape[1]
    near = pl.ds(pl.multiple_of(pick_ref[0] * half, half), half)
    for i, t in enumerate(turns):
        cols = pl.ds(pl.multiple_of(pick_ref[2 * t + 2] * BLOCK, BLOCK), BLOCK)

        @pl.when(pick_ref[2 * t + 1] == 0)
        def _(i=i, cols=cols):
            pltpu.make_async_copy(dlog_ref.at[near, cols], held.at[i], sem_in.at[i]).start()

        @pl.when(pick_ref[2 * t + 1] != 0)
        def _(i=i, cols=cols):
            pltpu.make_async_copy(sib_ref.at[near, cols], held.at[i], sem_in.at[i]).start()

    for i in range(n):
        pltpu.make_async_copy(sib_ref.at[near, pl.ds(0, BLOCK)], held.at[i], sem_in.at[i]).wait()
        pltpu.make_async_copy(held.at[i], outs[i], sem_out.at[i]).start()
    for i in range(n):
        pltpu.make_async_copy(held.at[i], outs[i], sem_out.at[i]).wait()


def pack(pick, dlog, sib, turns):
    half = dlog.shape[0] // 2
    n = len(turns)
    return pl.pallas_call(
        functools.partial(pack_kernel, turns),
        in_specs=[pl.BlockSpec(memory_space=pltpu.SMEM), HBM, HBM],
        out_specs=[HBM] * n,
        out_shape=[jax.ShapeDtypeStruct((half, BLOCK), BF16)] * n,
        scratch_shapes=[
            pltpu.VMEM((n, half, BLOCK), BF16),
            pltpu.SemaphoreType.DMA((n,)),
            pltpu.SemaphoreType.DMA((n,)),
        ],
        compiler_params=PARAMS,
        cost_estimate=cost(0, 4 * n * half * BLOCK),
        name="pack",
    )(pick, dlog, sib)


WORDS = 5


def fetch_whole(row, srcs, raw, sem, n):
    cols = pl.ds(pl.multiple_of(row(1) * BLOCK, BLOCK), BLOCK)
    copy = pltpu.make_async_copy(srcs[0].at[:, cols], raw.at[n], sem.at[2 * n])
    copy.start()
    return [copy]


def fetch_parts(row, srcs, raw, sem, n):
    half = raw.shape[1] // 2
    core = row(2)
    near = pl.ds(pl.multiple_of(core * half, half), half)
    far = pl.ds(pl.multiple_of((1 - core) * half, half), half)
    cols = pl.ds(pl.multiple_of(row(1) * BLOCK, BLOCK), BLOCK)

    def bring(near_src, far_src):
        pltpu.make_async_copy(near_src, raw.at[n, near], sem.at[2 * n]).start()
        pltpu.make_async_copy(far_src, raw.at[n, far], sem.at[2 * n + 1]).start()

    @pl.when(row(0) == 0)
    def _():
        bring(srcs[0].at[near, cols], srcs[0].at[far, cols])

    @pl.when(row(0) == 1)
    def _():
        bring(srcs[1].at[near, cols], srcs[1].at[far, cols])

    for t in range((len(srcs) - 2) // 2):

        @pl.when(row(0) == 2 + t)
        def _(t=t):
            bring(srcs[2 + 2 * t], srcs[3 + 2 * t])

    some = srcs[1].at[pl.ds(0, half), pl.ds(0, BLOCK)]
    return [
        pltpu.make_async_copy(some, raw.at[n, pl.ds(0, half)], sem.at[2 * n]),
        pltpu.make_async_copy(some, raw.at[n, pl.ds(half, half)], sem.at[2 * n + 1]),
    ]


def turn(plan, total, where_ref, at, srcs, sums, raw, turned, sem):
    waits = [plan(lambda w, m=m: where_ref[m * WORDS + w], srcs, raw, sem, n) for n, m in enumerate(at)]
    for n, m in enumerate(at):
        for wait in waits[n]:
            wait.wait()
        x = raw[n].astype(F32) * where_ref[m * WORDS + 3].astype(F32) - sums[n][0] / total
        turned[n * BLOCK : (n + 1) * BLOCK] = x.astype(BF16).T


def prepare_kernel(plan, total, n_src, at, where_ref, mask_ref, place_ref, own_ref, *refs):
    srcs, refs = refs[:n_src], refs[n_src:]
    energy_ref, sums_ref, dlog_ref, dener_ref, oc_ref, hc_ref, c_ref, h_ref, raw, turned, sem = refs
    t = pl.program_id(0)

    @pl.when(t == 0)
    def _():
        turn(plan, total, where_ref, [at], srcs, [own_ref], raw, turned, sem)

    on = mask_ref[place_ref[0] + t].astype(F32)
    ocf = dlog_ref[...].astype(F32) * on - sums_ref[0:1] / total
    oc = ocf.astype(BF16)
    shift = energy_ref[...] - sums_ref[2:3, 0:1] / total
    hc = (shift * ocf + dener_ref[...].astype(F32) * on - sums_ref[1:2] / total).astype(BF16)
    oc_ref[...] = oc
    hc_ref[...] = hc
    c_ref[...] = jnp.dot(turned[...], oc, preferred_element_type=F32).astype(BF16)
    h_ref[...] = jnp.dot(turned[...], hc, preferred_element_type=F32).astype(BF16)


def scratch(n_pos, rows):
    return [
        pltpu.VMEM((n_pos, rows, BLOCK), BF16),
        pltpu.VMEM((n_pos * BLOCK, rows), BF16),
        pltpu.SemaphoreType.DMA((2 * n_pos,)),
    ]


def prepare(plan, total, where, at, table, srcs, mask, place, energy, sums, dlog, dener):
    rows, width = dlog.shape
    block = pl.BlockSpec((rows, BLOCK), lambda t, *_: (0, t))
    one = pl.BlockSpec((BLOCK, BLOCK), lambda t, *_: (0, t))
    in_specs = [pl.BlockSpec((1, 1, BLOCK), lambda t, s, *_: (s[at * WORDS + 4], 0, 0))] + [HBM] * len(srcs)
    in_specs += [pl.BlockSpec((rows, 1), lambda t, *_: (0, 0))]
    in_specs += [pl.BlockSpec((sums.shape[0], BLOCK), lambda t, *_: (0, t))]
    return pl.pallas_call(
        functools.partial(prepare_kernel, plan, total, len(srcs), at),
        grid_spec=pltpu.PrefetchScalarGridSpec(
            num_scalar_prefetch=3,
            grid=(width // BLOCK,),
            in_specs=in_specs + [block, block],
            out_specs=[block, block, one, one],
            scratch_shapes=scratch(1, rows),
        ),
        out_shape=[jax.ShapeDtypeStruct((rows, width), BF16)] * 2 + [jax.ShapeDtypeStruct((BLOCK, width), BF16)] * 2,
        compiler_params=PARAMS,
        cost_estimate=cost(4 * BLOCK * rows * width, 8 * rows * width),
        name="prepare",
    )(where, mask, place, table, *srcs, energy, sums, dlog, dener)


def product_kernel(plan, total, n_src, at, kind, where_ref, *refs):
    n_pos = len(at)
    sums, srcs, refs = refs[:n_pos], refs[n_pos : n_pos + n_src], refs[n_pos + n_src :]
    oc_ref, hc_ref, refs = refs[0], refs[1], refs[2:]
    n_in = 0 if kind in ("first", "own") else n_pos
    arrived, refs = refs[:n_in], refs[n_in:]
    outs, (raw, turned, sem) = refs[:-3], refs[-3:]

    turn(plan, total, where_ref, at, srcs, sums, raw, turned, sem)
    lhs = turned[...]
    width = oc_ref.shape[1]
    tile = min(512, width)
    for start in range(0, width, tile):
        cols = slice(start, start + tile)
        c = jnp.dot(lhs, oc_ref[:, cols], preferred_element_type=F32)
        h = jnp.dot(lhs, hc_ref[:, cols], preferred_element_type=F32)
        if kind == "first":
            outs[0][:, cols] = c.astype(BF16)
            outs[1][:, cols] = h.astype(BF16)
            continue
        for n in range(n_pos):
            cn, hn = c[n * BLOCK : (n + 1) * BLOCK], h[n * BLOCK : (n + 1) * BLOCK]
            if kind == "add_c" or (kind == "second" and n == 0):
                cn = cn + arrived[n][:, cols].astype(F32)
            elif kind in ("add_h", "second"):
                hn = hn + arrived[n][:, cols].astype(F32)
            elif kind == "add":
                cn = cn + arrived[n][0, :, cols].astype(F32)
                hn = hn + arrived[n][1, :, cols].astype(F32)
            outs[n][0, :, cols] = cn.astype(outs[n].dtype)
            outs[n][1, :, cols] = hn.astype(outs[n].dtype)


def product(plan, total, where, at, table, srcs, oc, hc, kind, arrived=()):
    rows, width = oc.shape
    n_pos = len(at)
    in_specs = [pl.BlockSpec((1, 1, BLOCK), lambda t, s, m=m: (s[m * WORDS + 4], 0, 0)) for m in at]
    in_specs += [HBM] * len(srcs) + [VMEM] * (2 + len(arrived))
    if kind == "first":
        out_shape = [jax.ShapeDtypeStruct((BLOCK, width), BF16)] * 2
    else:
        out_shape = [jax.ShapeDtypeStruct((2, BLOCK, width), F32 if kind == "own" else BF16)] * n_pos
    return pl.pallas_call(
        functools.partial(product_kernel, plan, total, len(srcs), at, kind),
        grid_spec=pltpu.PrefetchScalarGridSpec(
            num_scalar_prefetch=1,
            grid=(1,),
            in_specs=in_specs,
            out_specs=[VMEM] * len(out_shape),
            scratch_shapes=scratch(n_pos, rows),
        ),
        out_shape=out_shape,
        compiler_params=SMALL,
        cost_estimate=cost(4 * n_pos * BLOCK * rows * width, 4 * rows * width + 8 * n_pos * BLOCK * width),
        name="product_" + kind,
    )(where, *[table] * n_pos, *srcs, oc, hc, *arrived)


def finish_kernel(total, own_ref, right_ref, left_ref, *refs):
    c_ref, h_ref = refs[-2:]
    c_ref[...] = (own_ref[0] + right_ref[0].astype(F32) + left_ref[0].astype(F32)) * (1.0 / total)
    h_ref[...] = (own_ref[1] + right_ref[1].astype(F32) + left_ref[1].astype(F32)) * (1.0 / total)


def finish(total, k, per_dest, own, right, left, so_far):
    _, rows, width = own.shape
    part = min(128, rows)
    two = pl.BlockSpec((2, part, width), lambda t: (0, t, 0))
    out = pl.BlockSpec((part, width), lambda t: (k * (rows // part) + t, 0))
    return pl.pallas_call(
        functools.partial(finish_kernel, total),
        grid=(rows // part,),
        in_specs=[two] * 3 + [HBM] * len(so_far),
        out_specs=[out, out],
        out_shape=[jax.ShapeDtypeStruct((per_dest * rows, width), F32)] * 2,
        input_output_aliases={3 + n: n for n in range(len(so_far))},
        compiler_params=PARAMS,
        cost_estimate=cost(6 * rows * width, 24 * rows * width),
        name="finish",
    )(own, right, left, *so_far)


def after(value, *others):
    return lax.optimization_barrier((value, *others))[0]


def sum_over_walk(x, nwalk, ties=()):
    if nwalk & (nwalk - 1):
        return lax.psum(x, "walk")
    step = 1
    while step < nwalk:
        if ties:
            x, ties = after(x, *ties[0]), ties[1:]
        x = x + lax.ppermute(x, "walk", [(w, w ^ step) for w in range(nwalk)])
        step *= 2
    return x


def per_device(dlog, dener, energy, mask, owner):
    wdev, width = dlog.shape
    nwalk, npan = lax.axis_size("walk"), lax.axis_size("pan")
    total = wdev * nwalk
    full = width * npan
    nblocks = full // BLOCK
    mine = width // BLOCK
    per_dest = nblocks // nwalk
    half = nwalk // 2
    pan, walk = lax.axis_index("pan"), lax.axis_index("walk")

    ring = [2 * k for k in range(half)] + [2 * k + 1 for k in reversed(range(half))]
    right = [(ring[k], ring[(k + 1) % nwalk]) for k in range(nwalk)]
    left = [(b, a) for a, b in right]
    spot = jnp.where(walk % 2 == 0, walk // 2, nwalk - 1 - walk // 2)

    offsets = [(half, k) for k in range(per_dest)]
    for j in range(half - 1, 0, -1):
        for k in range(per_dest):
            offsets += [(j, k), (-j, k)]
    offsets += [(0, k) for k in range(per_dest)]
    goal = (spot + jnp.array([o for o, _ in offsets], jnp.int32)) % nwalk
    goal = jnp.where(goal < half, 2 * goal, 2 * (nwalk - 1 - goal) + 1)
    position = goal * per_dest + jnp.array([k for _, k in offsets], jnp.int32)
    wanted = owner[position]
    shown = mask[wanted]
    place = (pan * mine)[None].astype(jnp.int32)
    column = energy[:, None]
    made = []

    if npan == 4:
        chip, core = pan // 2, pan % 2
        swap = [(j, j ^ 1) for j in range(npan)]
        cross = [(j, j ^ 2) for j in range(npan)]
        rounds = 2 * mine
        sib = lax.ppermute(dlog, "pan", swap)
        here = wanted // rounds == chip
        rank_here = jnp.cumsum(here) - 1
        rank_there = jnp.cumsum(~here) - 1
        turns = jnp.arange(rounds)[:, None]
        picked = jnp.sum(jnp.where(here & (rank_here == turns), wanted, 0), 1)
        pick = jnp.stack([jnp.where(picked // mine == pan, 0, 1), picked % mine], 1).reshape(-1)
        pick = jnp.concatenate([core[None], pick]).astype(jnp.int32)
        sums = column_sums(mask, after(place, pick), energy, dlog, dener)
        sums = jnp.concatenate([sums[:3], lax.ppermute(sums[:1], "pan", cross)])
        sends = pack(after(pick, sums), dlog, sib, tuple(range(rounds)))
        crossed = [lax.ppermute(send, "pan", cross) for send in sends]
        sums = sum_over_walk(sums, nwalk, [crossed[:1], (), crossed[1:2]])
        pair = jnp.stack([sums[0], sums[3]])
        table = jnp.concatenate([pair, lax.ppermute(pair, "pan", swap)])
        there = wanted // mine
        entry = ((there % 2 != core) * 2 + (there // 2 != chip)) * mine + wanted % mine
        kind = jnp.where(here, jnp.where(wanted // mine == pan, 0, 1), 2 + rank_there)
        where = jnp.stack([kind, wanted % mine, jnp.full_like(wanted, core), shown, entry], 1)
        plan = fetch_parts
        parts = []

        def sources(m):
            for t in range(len(parts) // 2, min(m + 1, rounds)):
                tie = {0: None, 1: table}.get(t, made[max(t - 2, 0)] if t >= 2 else None)
                got = crossed[t] if tie is None else after(crossed[t], tie)
                parts.extend([got, lax.ppermute(got, "pan", swap)])
            return [dlog, sib] + parts[: 2 * min(m + 1, rounds)]
    else:
        gathered = lax.all_gather(dlog, "pan", axis=1, tiled=True)
        sums = sum_over_walk(column_sums(mask, place, energy, dlog, dener), nwalk)
        table = lax.all_gather(sums[0], "pan")
        where = jnp.stack([wanted, wanted, wanted, shown, wanted], 1)
        plan = fetch_whole

        def sources(m):
            return [gathered]

    where = where.astype(jnp.int32).reshape(-1)
    table = table.reshape(nblocks, 1, BLOCK)
    oc, hc, first_c, first_h = prepare(
        plan, total, where, 0, table, sources(0), mask, place, column, sums, dlog, dener
    )
    made.append(first_c)
    index = {key: m for m, key in enumerate(offsets)}

    def run(keys, kind, *arrived):
        at = [index[key] for key in keys]
        outs = product(plan, total, where, at, table, sources(max(at)), oc, hc, kind, arrived)
        made.extend(outs[: len(at)])
        return outs

    moving_right, moving_left = {}, {}
    for k in range(per_dest):
        c, h = run([(half, k)], "first") if k else (first_c, first_h)
        moving_right[k] = lax.ppermute(c, "walk", right)
        moving_left[k] = lax.ppermute(h, "walk", left)
    for j in range(half - 1, 0, -1):
        for k in range(per_dest):
            one = j == half - 1
            if index[j, k] < 2 * mine:
                (r,) = run([(j, k)], "add_c" if one else "add", moving_right[k])
                moving_right[k] = lax.ppermute(r, "walk", right)
                (l,) = run([(-j, k)], "add_h" if one else "add", moving_left[k])
                moving_left[k] = lax.ppermute(l, "walk", left)
            else:
                r, l = run([(j, k), (-j, k)], "second" if one else "add", moving_right[k], moving_left[k])
                moving_right[k] = lax.ppermute(r, "walk", right)
                moving_left[k] = lax.ppermute(l, "walk", left)
    own = run([(0, k) for k in range(per_dest)], "own")
    outs = ()
    for k in range(per_dest):
        outs = finish(total, k, per_dest, own[k], moving_right[k], moving_left[k], outs)
    return tuple(outs)


def solution(mesh):
    return jax.shard_map(
        per_device,
        mesh=mesh,
        in_specs=(P("walk", "pan"), P("walk", "pan"), P("walk"), P(), P()),
        out_specs=(P("walk", "pan"), P("walk", "pan")),
        check_vma=False,
    )
```

```python
import functools

import jax
import jax.numpy as jnp
from jax import lax
from jax.experimental import pallas as pl
from jax.experimental.pallas import tpu as pltpu
from jax.sharding import PartitionSpec as P

BLOCK = 256
VMEM_LIMIT = 56 * 1024 * 1024
F32 = jnp.float32
BF16 = jnp.bfloat16
PARAMS = pltpu.CompilerParams(vmem_limit_bytes=VMEM_LIMIT)
SMALL = pltpu.CompilerParams(vmem_limit_bytes=32 * 1024 * 1024)
HBM = pl.BlockSpec(memory_space=pltpu.HBM)
VMEM = pl.BlockSpec(memory_space=pltpu.VMEM)


def cost(flops, moved):
    return pl.CostEstimate(flops=flops // 100, bytes_accessed=moved // 100, transcendentals=0)


def sums_kernel(mask_ref, place_ref, energy_ref, dlog_ref, dener_ref, out_ref):
    on = mask_ref[place_ref[0] + pl.program_id(0)].astype(F32)
    out_ref[0:1] = jnp.sum(dlog_ref[...].astype(F32) * on, 0, keepdims=True)
    out_ref[1:2] = jnp.sum(dener_ref[...].astype(F32) * on, 0, keepdims=True)
    out_ref[2:8] = jnp.full((6, out_ref.shape[1]), jnp.sum(energy_ref[...]), F32)


def column_sums(mask, place, energy, dlog, dener):
    rows, width = dlog.shape
    block = pl.BlockSpec((rows, BLOCK), lambda t, *_: (0, t))
    energy = energy.reshape(rows // 128, 128)
    return pl.pallas_call(
        sums_kernel,
        grid_spec=pltpu.PrefetchScalarGridSpec(
            num_scalar_prefetch=2,
            grid=(width // BLOCK,),
            in_specs=[pl.BlockSpec(energy.shape, lambda t, *_: (0, 0)), block, block],
            out_specs=pl.BlockSpec((8, BLOCK), lambda t, *_: (0, t)),
        ),
        out_shape=jax.ShapeDtypeStruct((8, width), F32),
        compiler_params=PARAMS,
        cost_estimate=cost(4 * rows * width, 4 * rows * width),
        name="column_sums",
    )(mask, place, energy, dlog, dener)


def pack_kernel(turns, pick_ref, dlog_ref, sib_ref, *refs):
    n = len(turns)
    outs, (held, sem_in, sem_out) = refs[:n], refs[n:]
    half = held.shape[1]
    near = pl.ds(pl.multiple_of(pick_ref[0] * half, half), half)
    for i, t in enumerate(turns):
        cols = pl.ds(pl.multiple_of(pick_ref[2 * t + 2] * BLOCK, BLOCK), BLOCK)

        @pl.when(pick_ref[2 * t + 1] == 0)
        def _(i=i, cols=cols):
            pltpu.make_async_copy(dlog_ref.at[near, cols], held.at[i], sem_in.at[i]).start()

        @pl.when(pick_ref[2 * t + 1] != 0)
        def _(i=i, cols=cols):
            pltpu.make_async_copy(sib_ref.at[near, cols], held.at[i], sem_in.at[i]).start()

    for i in range(n):
        pltpu.make_async_copy(sib_ref.at[near, pl.ds(0, BLOCK)], held.at[i], sem_in.at[i]).wait()
        pltpu.make_async_copy(held.at[i], outs[i], sem_out.at[i]).start()
    for i in range(n):
        pltpu.make_async_copy(held.at[i], outs[i], sem_out.at[i]).wait()


def pack(pick, dlog, sib, turns):
    half = dlog.shape[0] // 2
    n = len(turns)
    return pl.pallas_call(
        functools.partial(pack_kernel, turns),
        in_specs=[pl.BlockSpec(memory_space=pltpu.SMEM), HBM, HBM],
        out_specs=[HBM] * n,
        out_shape=[jax.ShapeDtypeStruct((half, BLOCK), BF16)] * n,
        scratch_shapes=[
            pltpu.VMEM((n, half, BLOCK), BF16),
            pltpu.SemaphoreType.DMA((n,)),
            pltpu.SemaphoreType.DMA((n,)),
        ],
        compiler_params=PARAMS,
        cost_estimate=cost(0, 4 * n * half * BLOCK),
        name="pack",
    )(pick, dlog, sib)


WORDS = 5


def fetch_whole(row, srcs, raw, sem, n):
    cols = pl.ds(pl.multiple_of(row(1) * BLOCK, BLOCK), BLOCK)
    copy = pltpu.make_async_copy(srcs[0].at[:, cols], raw.at[n], sem.at[2 * n])
    copy.start()
    return [copy]


def fetch_parts(row, srcs, raw, sem, n):
    half = raw.shape[1] // 2
    core = row(2)
    near = pl.ds(pl.multiple_of(core * half, half), half)
    far = pl.ds(pl.multiple_of((1 - core) * half, half), half)
    cols = pl.ds(pl.multiple_of(row(1) * BLOCK, BLOCK), BLOCK)

    def bring(near_src, far_src):
        pltpu.make_async_copy(near_src, raw.at[n, near], sem.at[2 * n]).start()
        pltpu.make_async_copy(far_src, raw.at[n, far], sem.at[2 * n + 1]).start()

    @pl.when(row(0) == 0)
    def _():
        bring(srcs[0].at[near, cols], srcs[0].at[far, cols])

    @pl.when(row(0) == 1)
    def _():
        bring(srcs[1].at[near, cols], srcs[1].at[far, cols])

    for t in range((len(srcs) - 2) // 2):

        @pl.when(row(0) == 2 + t)
        def _(t=t):
            bring(srcs[2 + 2 * t], srcs[3 + 2 * t])

    some = srcs[1].at[pl.ds(0, half), pl.ds(0, BLOCK)]
    return [
        pltpu.make_async_copy(some, raw.at[n, pl.ds(0, half)], sem.at[2 * n]),
        pltpu.make_async_copy(some, raw.at[n, pl.ds(half, half)], sem.at[2 * n + 1]),
    ]


def turn(plan, total, where_ref, at, srcs, sums, raw, turned, sem):
    waits = [plan(lambda w, m=m: where_ref[m * WORDS + w], srcs, raw, sem, n) for n, m in enumerate(at)]
    for n, m in enumerate(at):
        for wait in waits[n]:
            wait.wait()
        x = raw[n].astype(F32) * where_ref[m * WORDS + 3].astype(F32) - sums[n][0] / total
        turned[n * BLOCK : (n + 1) * BLOCK] = x.astype(BF16).T


def prepare_kernel(plan, total, n_src, at, where_ref, mask_ref, place_ref, own_ref, *refs):
    srcs, refs = refs[:n_src], refs[n_src:]
    energy_ref, sums_ref, dlog_ref, dener_ref, oc_ref, hc_ref, c_ref, h_ref, raw, turned, sem = refs
    t = pl.program_id(0)

    @pl.when(t == 0)
    def _():
        turn(plan, total, where_ref, [at], srcs, [own_ref], raw, turned, sem)

    on = mask_ref[place_ref[0] + t].astype(F32)
    ocf = dlog_ref[...].astype(F32) * on - sums_ref[0:1] / total
    oc = ocf.astype(BF16)
    shift = energy_ref[...] - sums_ref[2:3, 0:1] / total
    hc = (shift * ocf + dener_ref[...].astype(F32) * on - sums_ref[1:2] / total).astype(BF16)
    oc_ref[...] = oc
    hc_ref[...] = hc
    c_ref[...] = jnp.dot(turned[...], oc, preferred_element_type=F32).astype(BF16)
    h_ref[...] = jnp.dot(turned[...], hc, preferred_element_type=F32).astype(BF16)


def scratch(n_pos, rows):
    return [
        pltpu.VMEM((n_pos, rows, BLOCK), BF16),
        pltpu.VMEM((n_pos * BLOCK, rows), BF16),
        pltpu.SemaphoreType.DMA((2 * n_pos,)),
    ]


def prepare(plan, total, where, at, table, srcs, mask, place, energy, sums, dlog, dener):
    rows, width = dlog.shape
    block = pl.BlockSpec((rows, BLOCK), lambda t, *_: (0, t))
    one = pl.BlockSpec((BLOCK, BLOCK), lambda t, *_: (0, t))
    in_specs = [pl.BlockSpec((1, 1, BLOCK), lambda t, s, *_: (s[at * WORDS + 4], 0, 0))] + [HBM] * len(srcs)
    in_specs += [pl.BlockSpec((rows, 1), lambda t, *_: (0, 0))]
    in_specs += [pl.BlockSpec((sums.shape[0], BLOCK), lambda t, *_: (0, t))]
    return pl.pallas_call(
        functools.partial(prepare_kernel, plan, total, len(srcs), at),
        grid_spec=pltpu.PrefetchScalarGridSpec(
            num_scalar_prefetch=3,
            grid=(width // BLOCK,),
            in_specs=in_specs + [block, block],
            out_specs=[block, block, one, one],
            scratch_shapes=scratch(1, rows),
        ),
        out_shape=[jax.ShapeDtypeStruct((rows, width), BF16)] * 2 + [jax.ShapeDtypeStruct((BLOCK, width), BF16)] * 2,
        compiler_params=PARAMS,
        cost_estimate=cost(4 * BLOCK * rows * width, 8 * rows * width),
        name="prepare",
    )(where, mask, place, table, *srcs, energy, sums, dlog, dener)


def product_kernel(plan, total, n_src, at, kind, where_ref, *refs):
    n_pos = len(at)
    sums, srcs, refs = refs[:n_pos], refs[n_pos : n_pos + n_src], refs[n_pos + n_src :]
    oc_ref, hc_ref, refs = refs[0], refs[1], refs[2:]
    n_in = 0 if kind in ("first", "own") else n_pos
    arrived, refs = refs[:n_in], refs[n_in:]
    outs, (raw, turned, sem) = refs[:-3], refs[-3:]

    turn(plan, total, where_ref, at, srcs, sums, raw, turned, sem)
    lhs = turned[...]
    width = oc_ref.shape[1]
    tile = min(512, width)
    for start in range(0, width, tile):
        cols = slice(start, start + tile)
        c = jnp.dot(lhs, oc_ref[:, cols], preferred_element_type=F32)
        h = jnp.dot(lhs, hc_ref[:, cols], preferred_element_type=F32)
        if kind == "first":
            outs[0][:, cols] = c.astype(BF16)
            outs[1][:, cols] = h.astype(BF16)
            continue
        for n in range(n_pos):
            cn, hn = c[n * BLOCK : (n + 1) * BLOCK], h[n * BLOCK : (n + 1) * BLOCK]
            if kind == "add_c" or (kind == "second" and n == 0):
                cn = cn + arrived[n][:, cols].astype(F32)
            elif kind in ("add_h", "second"):
                hn = hn + arrived[n][:, cols].astype(F32)
            elif kind == "add":
                cn = cn + arrived[n][0, :, cols].astype(F32)
                hn = hn + arrived[n][1, :, cols].astype(F32)
            outs[n][0, :, cols] = cn.astype(outs[n].dtype)
            outs[n][1, :, cols] = hn.astype(outs[n].dtype)


def product(plan, total, where, at, table, srcs, oc, hc, kind, arrived=()):
    rows, width = oc.shape
    n_pos = len(at)
    in_specs = [pl.BlockSpec((1, 1, BLOCK), lambda t, s, m=m: (s[m * WORDS + 4], 0, 0)) for m in at]
    in_specs += [HBM] * len(srcs) + [VMEM] * (2 + len(arrived))
    if kind == "first":
        out_shape = [jax.ShapeDtypeStruct((BLOCK, width), BF16)] * 2
    else:
        out_shape = [jax.ShapeDtypeStruct((2, BLOCK, width), F32 if kind == "own" else BF16)] * n_pos
    return pl.pallas_call(
        functools.partial(product_kernel, plan, total, len(srcs), at, kind),
        grid_spec=pltpu.PrefetchScalarGridSpec(
            num_scalar_prefetch=1,
            grid=(1,),
            in_specs=in_specs,
            out_specs=[VMEM] * len(out_shape),
            scratch_shapes=scratch(n_pos, rows),
        ),
        out_shape=out_shape,
        compiler_params=SMALL,
        cost_estimate=cost(4 * n_pos * BLOCK * rows * width, 4 * rows * width + 8 * n_pos * BLOCK * width),
        name="product_" + kind,
    )(where, *[table] * n_pos, *srcs, oc, hc, *arrived)


def finish_kernel(total, own_ref, right_ref, left_ref, *refs):
    c_ref, h_ref = refs[-2:]
    c_ref[...] = (own_ref[0] + right_ref[0].astype(F32) + left_ref[0].astype(F32)) * (1.0 / total)
    h_ref[...] = (own_ref[1] + right_ref[1].astype(F32) + left_ref[1].astype(F32)) * (1.0 / total)


def finish(total, k, per_dest, own, right, left, so_far):
    _, rows, width = own.shape
    part = min(32, rows)
    two = pl.BlockSpec((2, part, width), lambda t: (0, t, 0))
    out = pl.BlockSpec((part, width), lambda t: (k * (rows // part) + t, 0))
    return pl.pallas_call(
        functools.partial(finish_kernel, total),
        grid=(rows // part,),
        in_specs=[two] * 3 + [HBM] * len(so_far),
        out_specs=[out, out],
        out_shape=[jax.ShapeDtypeStruct((per_dest * rows, width), F32)] * 2,
        input_output_aliases={3 + n: n for n in range(len(so_far))},
        compiler_params=PARAMS,
        cost_estimate=cost(6 * rows * width, 24 * rows * width),
        name="finish",
    )(own, right, left, *so_far)


def after(value, *others):
    return lax.optimization_barrier((value, *others))[0]


def sum_over_walk(x, nwalk, ties=()):
    if nwalk & (nwalk - 1):
        return lax.psum(x, "walk")
    step = 1
    while step < nwalk:
        if ties:
            x, ties = after(x, *ties[0]), ties[1:]
        x = x + lax.ppermute(x, "walk", [(w, w ^ step) for w in range(nwalk)])
        step *= 2
    return x


def per_device(dlog, dener, energy, mask, owner):
    wdev, width = dlog.shape
    nwalk, npan = lax.axis_size("walk"), lax.axis_size("pan")
    total = wdev * nwalk
    full = width * npan
    nblocks = full // BLOCK
    mine = width // BLOCK
    per_dest = nblocks // nwalk
    half = nwalk // 2
    pan, walk = lax.axis_index("pan"), lax.axis_index("walk")

    ring = [2 * k for k in range(half)] + [2 * k + 1 for k in reversed(range(half))]
    right = [(ring[k], ring[(k + 1) % nwalk]) for k in range(nwalk)]
    left = [(b, a) for a, b in right]
    spot = jnp.where(walk % 2 == 0, walk // 2, nwalk - 1 - walk // 2)

    offsets = [(half, k) for k in range(per_dest)]
    for j in range(half - 1, 0, -1):
        for k in range(per_dest):
            offsets += [(j, k), (-j, k)]
    offsets += [(0, k) for k in range(per_dest)]
    goal = (spot + jnp.array([o for o, _ in offsets], jnp.int32)) % nwalk
    goal = jnp.where(goal < half, 2 * goal, 2 * (nwalk - 1 - goal) + 1)
    position = goal * per_dest + jnp.array([k for _, k in offsets], jnp.int32)
    wanted = owner[position]
    shown = mask[wanted]
    place = (pan * mine)[None].astype(jnp.int32)
    column = energy[:, None]
    made = []

    if npan == 4:
        chip, core = pan // 2, pan % 2
        swap = [(j, j ^ 1) for j in range(npan)]
        cross = [(j, j ^ 2) for j in range(npan)]
        rounds = 2 * mine
        sib = lax.ppermute(dlog, "pan", swap)
        here = wanted // rounds == chip
        rank_here = jnp.cumsum(here) - 1
        rank_there = jnp.cumsum(~here) - 1
        turns = jnp.arange(rounds)[:, None]
        picked = jnp.sum(jnp.where(here & (rank_here == turns), wanted, 0), 1)
        pick = jnp.stack([jnp.where(picked // mine == pan, 0, 1), picked % mine], 1).reshape(-1)
        pick = jnp.concatenate([core[None], pick]).astype(jnp.int32)
        sums = column_sums(mask, after(place, pick), energy, dlog, dener)
        sums = jnp.concatenate([sums[:3], lax.ppermute(sums[:1], "pan", cross)])
        sends = pack(after(pick, sums), dlog, sib, tuple(range(rounds)))
        crossed = [lax.ppermute(send, "pan", cross) for send in sends]
        sums = sum_over_walk(sums, nwalk, [crossed[:1], (), crossed[1:2]])
        pair = jnp.stack([sums[0], sums[3]])
        table = jnp.concatenate([pair, lax.ppermute(pair, "pan", swap)])
        there = wanted // mine
        entry = ((there % 2 != core) * 2 + (there // 2 != chip)) * mine + wanted % mine
        kind = jnp.where(here, jnp.where(wanted // mine == pan, 0, 1), 2 + rank_there)
        where = jnp.stack([kind, wanted % mine, jnp.full_like(wanted, core), shown, entry], 1)
        plan = fetch_parts
        parts = []

        def sources(m):
            for t in range(len(parts) // 2, min(m + 1, rounds)):
                tie = {0: None, 1: table}.get(t, made[max(t - 2, 0)] if t >= 2 else None)
                got = crossed[t] if tie is None else after(crossed[t], tie)
                parts.extend([got, lax.ppermute(got, "pan", swap)])
            return [dlog, sib] + parts[: 2 * min(m + 1, rounds)]
    else:
        gathered = lax.all_gather(dlog, "pan", axis=1, tiled=True)
        sums = sum_over_walk(column_sums(mask, place, energy, dlog, dener), nwalk)
        table = lax.all_gather(sums[0], "pan")
        where = jnp.stack([wanted, wanted, wanted, shown, wanted], 1)
        plan = fetch_whole

        def sources(m):
            return [gathered]

    where = where.astype(jnp.int32).reshape(-1)
    table = table.reshape(nblocks, 1, BLOCK)
    oc, hc, first_c, first_h = prepare(
        plan, total, where, 0, table, sources(0), mask, place, column, sums, dlog, dener
    )
    made.append(first_c)
    index = {key: m for m, key in enumerate(offsets)}

    def run(keys, kind, *arrived):
        at = [index[key] for key in keys]
        outs = product(plan, total, where, at, table, sources(max(at)), oc, hc, kind, arrived)
        made.extend(outs[: len(at)])
        return outs

    moving_right, moving_left = {}, {}
    for k in range(per_dest):
        c, h = run([(half, k)], "first") if k else (first_c, first_h)
        moving_right[k] = lax.ppermute(c, "walk", right)
        moving_left[k] = lax.ppermute(h, "walk", left)
    for j in range(half - 1, 0, -1):
        for k in range(per_dest):
            one = j == half - 1
            if index[j, k] < 2 * mine:
                (r,) = run([(j, k)], "add_c" if one else "add", moving_right[k])
                moving_right[k] = lax.ppermute(r, "walk", right)
                (l,) = run([(-j, k)], "add_h" if one else "add", moving_left[k])
                moving_left[k] = lax.ppermute(l, "walk", left)
            else:
                r, l = run([(j, k), (-j, k)], "second" if one else "add", moving_right[k], moving_left[k])
                moving_right[k] = lax.ppermute(r, "walk", right)
                moving_left[k] = lax.ppermute(l, "walk", left)
    own = run([(0, k) for k in range(per_dest)], "own")
    outs = ()
    for k in range(per_dest):
        outs = finish(total, k, per_dest, own[k], moving_right[k], moving_left[k], outs)
    return tuple(outs)


def solution(mesh):
    return jax.shard_map(
        per_device,
        mesh=mesh,
        in_specs=(P("walk", "pan"), P("walk", "pan"), P("walk"), P(), P()),
        out_specs=(P("walk", "pan"), P("walk", "pan")),
        check_vma=False,
    )
```
